256 devices in a mesh: dp: 32 (over z, x), tensor: 8 (over y, core).
Axes of the slice: x: 4, y: 4, z: 8, core: 2. Of those that a mesh axis runs over, the one named last changes fastest.
Arguments:
- momentum: float32 [32, 256, 28672], P('dp', None, 'tensor')
- gradient: bfloat16 [32, 256, 28672], P('dp', None, 'tensor'), may hold values from -6 to 6
- kept: int32 [32, 4, 448, 32], P('dp', None, 'tensor'), may hold values from 0 to 4095, as said below
Outputs:
- update: float32 [256, 28672], P(None, 'tensor')
- new_momentum: float32 [32, 256, 28672], P('dp', None, 'tensor')
The draws below stay inside these ranges and needn't reach their ends.
Inputs may be any that keep to these rules, and one draw needn't show every extreme that they name: Sorted, the i-th kept index of a block lies in [i * 64 * 2, (i + 1) * 64 * 2); the kept indices of a block are distinct.
All inputs are finite; a program needn't handle non-finite values.
Results may differ from the reference program's by a relative error of at most 0.0003.
Values sent between devices are 32-bit elements; how exact they have to be, the bound alone decides.
No kernel may reach another device: no remote copies, remote signals or barrier semaphores. Data moves between devices by JAX's collectives and lax.ppermute only.
A program may use at most 128 MiB of HBM per device.

```python
import jax
import jax.numpy as jnp
from jax import lax

FF = 28672
ROWS = 256
BLK = 64
KEEP = 32
REPLICAS = 32


def draw_kept(key, part):
    key = jax.random.fold_in(key, 1)
    band = BLK * BLK // KEEP
    offsets = jax.random.randint(key, (REPLICAS, ROWS // BLK, FF // BLK, KEEP), 0, band, dtype=jnp.int32)
    return offsets + jnp.arange(KEEP, dtype=jnp.int32) * band


def draw_momentum(key, part):
    key = jax.random.fold_in(key, 2)
    key_base, key_rows, key_cols = jax.random.split(key, 3)
    row_scale = jnp.exp(jax.random.uniform(key_rows, (REPLICAS, ROWS, 1), jnp.float32, jnp.log(0.3), jnp.log(3.0)))
    col_scale = jnp.exp(jax.random.uniform(key_cols, (1, 1, FF), jnp.float32, jnp.log(0.3), jnp.log(3.0)))
    base = jax.random.normal(key_base, (REPLICAS, ROWS, FF), jnp.float32)
    return (base * row_scale * col_scale).astype(jnp.float32)


def steps_of(key, extent, cuts, least, high):
    factor_of = 1.0
    for dim, shards_of in cuts:
        steps = jax.random.uniform(jax.random.fold_in(jax.random.fold_in(key, 6), dim), (shards_of,), jnp.float32, least / len(cuts), high / len(cuts))
        factor_of = factor_of * jnp.repeat(jnp.exp(steps), extent[dim] // shards_of).reshape((-1,) + (1,) * (len(extent) - 1 - dim))
    return factor_of


def centred(key, shape, spread, most, shards=(), kind=jnp.bfloat16):
    values = jax.random.normal(key, shape, jnp.float32) * spread
    if len(shards) > 0:
        values = steps_of(key, shape, shards, -0.22, 0.18) * values
    return jnp.clip(values, min=-most, max=most).astype(kind)


def setup_inputs(seed: int = 0) -> dict:
    key_list = jax.random.split(jax.random.key(seed), 4)
    momentum = draw_momentum(jax.random.fold_in(key_list[3], 71), 0)
    gradient = centred(key_list[1], (REPLICAS, ROWS, FF), 1.0, 6.0, ((0, 32), (2, 8)))
    kept = draw_kept(jax.random.fold_in(key_list[3], 71), 0)
    return dict(momentum=momentum, gradient=gradient, kept=kept)


decay_rate = 0.9
epsilon = 1e-06

def cosine_matrix():
    freqs = jnp.arange(BLK, dtype=jnp.float32)[:, None]
    cells = jnp.arange(BLK, dtype=jnp.float32)[None, :]
    matrix = jnp.cos(jnp.pi * (2.0 * cells + 1.0) * freqs / (2.0 * BLK)) * jnp.sqrt(2.0 / BLK)
    first = jnp.where(jnp.arange(BLK)[:, None] == 0, 1.0 / jnp.sqrt(2.0), 1.0).astype(jnp.float32)
    return matrix * first

def forward(field, cosine):
    blocks = field.reshape(field.shape[0] // BLK, BLK, field.shape[1] // BLK, BLK)
    coeffs = jnp.einsum('ia,paqb,jb->pqij', cosine, blocks, cosine, precision=lax.Precision.HIGHEST)
    return coeffs.reshape(coeffs.shape[0], coeffs.shape[1], BLK * BLK)

def inverse(coeffs, cosine):
    blocks = coeffs.reshape(coeffs.shape[0], coeffs.shape[1], BLK, BLK)
    field = jnp.einsum('ia,pqij,jb->paqb', cosine, blocks, cosine, precision=lax.Precision.HIGHEST)
    return field.reshape(coeffs.shape[0] * BLK, coeffs.shape[1] * BLK)

def place(total, values, places):
    rows_idx = jnp.arange(total.shape[0], dtype=jnp.int32)[:, None, None]
    cols_idx = jnp.arange(total.shape[1], dtype=jnp.int32)[None, :, None]
    return total.at[rows_idx, cols_idx, places].add(values)

def reference(momentum, gradient, kept):
    cosine = cosine_matrix()
    zeros_coeff = jnp.zeros((ROWS // BLK, FF // BLK, BLK * BLK), jnp.float32)

    def replica(summed, inputs):
        mom_one, grad_one, places = inputs
        accumulated = decay_rate * mom_one + grad_one.astype(jnp.float32)
        coeffs = forward(accumulated, cosine)
        values = jnp.take_along_axis(coeffs, places, axis=-1)
        sparse = place(zeros_coeff, values, places)
        residual = accumulated - inverse(sparse, cosine)
        return (summed + sparse, residual)
    summed, new_momentum = lax.scan(replica, zeros_coeff, (momentum, gradient, kept))
    combined = inverse(summed, cosine)
    mean_square = jnp.sum(combined * combined) / (ROWS * FF)
    update = combined / jnp.sqrt(mean_square + epsilon)
    return (update, new_momentum)
```

```python
import functools

import jax
import jax.numpy as jnp
import numpy as np
from jax import lax
from jax.experimental import pallas as pl
from jax.experimental.pallas import tpu as pltpu
from jax.sharding import PartitionSpec as P

FF = 28672
ROWS = 256
BLK = 64
KEEP = 32
BAND = BLK * BLK // KEEP
TILE = 256
WIDE = 512

decay_rate = 0.9
epsilon = 1e-06


def thirds_np(x):
    high = x.astype(jnp.bfloat16)
    low = (x - high.astype(np.float32)).astype(jnp.bfloat16)
    return np.concatenate([high, low, high])


def constants():
    k = np.arange(BLK)[:, None]
    n = np.arange(BLK)[None, :]
    c = np.cos(np.pi * (2.0 * n + 1.0) * k / (2.0 * BLK)) * np.sqrt(2.0 / BLK)
    c[0] *= 1.0 / np.sqrt(2.0)
    right = np.kron(np.eye(4), c).astype(np.float32)
    order = [p * BLK + 2 * i + h for h in range(2) for p in range(4) for i in range(KEEP)]
    left = right[order]
    forward = np.stack([thirds_np(right.T), thirds_np(left.T)])
    inverse = np.stack([thirds_np(left), thirds_np(right)])
    return forward, inverse


def dot3(x, thirds):
    high = x.astype(jnp.bfloat16)
    low = (x - high.astype(jnp.float32)).astype(jnp.bfloat16)
    return jnp.dot(jnp.concatenate([high, high, low], axis=1), thirds, preferred_element_type=jnp.float32)


def rows_of(q):
    return slice(q * BLK, (q + 1) * BLK)


def values_kernel(m_ref, g_ref, e_ref, c_ref, v_ref):
    cells = lax.broadcasted_iota(jnp.int32, (BLK, 128), 0)
    for s in range(WIDE // TILE):
        cols = slice(s * TILE, (s + 1) * TILE)
        acc = decay_rate * m_ref[0, :, cols] + g_ref[0, :, cols].astype(jnp.float32)
        coeffs = dot3(dot3(acc, c_ref[0]).T, c_ref[1])
        for q in range(4):
            row = s * 4 + q
            e = e_ref[row : row + 1, :]
            block = coeffs[rows_of(q)]
            chosen = jnp.where(e == cells, block[:, :128], 0.0) + jnp.where(e == cells + BLK, block[:, 128:], 0.0)
            v_ref[row : row + 1, :] = jnp.sum(chosen, axis=0, keepdims=True)


def inverse_tile(sparse_t, c_ref):
    return dot3(dot3(sparse_t, c_ref[0]).T, c_ref[1])


def residual_kernel(m_ref, g_ref, e_ref, v_ref, c_ref, *rest):
    o_ref = rest[-1]
    cells = lax.broadcasted_iota(jnp.int32, (BLK, 128), 0)
    for s in range(WIDE // TILE):
        cols = slice(s * TILE, (s + 1) * TILE)
        parts = []
        for q in range(4):
            row = s * 4 + q
            e = e_ref[row : row + 1, :]
            v = v_ref[row : row + 1, :]
            even = jnp.where(e == cells, v, 0.0)
            odd = jnp.where(e == cells + BLK, v, 0.0)
            parts.append(jnp.concatenate([even, odd], axis=1))
        field = inverse_tile(jnp.concatenate(parts, axis=0), c_ref)
        acc = decay_rate * m_ref[0, :, cols] + g_ref[0, :, cols].astype(jnp.float32)
        o_ref[0, :, cols] = acc - field


def merge_kernel(*refs):
    *parts, place_ref, total_ref, sq_ref = refs
    count = len(parts) // 2
    each = parts[0].shape[0]

    def rows(g, squares):
        at = pl.ds(pl.multiple_of(g * 8, 8), 8)
        places = [ref[r, at, :] for ref in parts[:count] for r in range(each)]
        totals = [ref[r, at, :] for ref in parts[count:] for r in range(each)]
        for i in range(len(places)):
            place, total = places[i], totals[i]
            for j in range(i + 1, len(places)):
                same = place == places[j]
                total = total + jnp.where(same, totals[j], 0.0)
                places[j] = jnp.where(same, -1 - j, places[j])
            place_ref[i, at, :] = place
            total_ref[i, at, :] = total
            squares = squares + jnp.where(place >= 0, total * total, 0.0)
        return squares

    sq_ref[...] = lax.fori_loop(0, place_ref.shape[1] // 8, rows, jnp.zeros((8, 128), jnp.float32))


def combined_kernel(e_ref, v_ref, c_ref, o_ref):
    step = pl.program_id(0)
    cells = lax.broadcasted_iota(jnp.int32, (BLK, 128), 0)
    cells2 = cells + BLK
    per = WIDE // BLK
    for s in range(WIDE // TILE):
        parts = []
        for q in range(4):
            row = pl.ds(step * per + s * 4 + q, 1)
            even = jnp.zeros((BLK, 128), jnp.float32)
            odd = jnp.zeros((BLK, 128), jnp.float32)
            for r in range(e_ref.shape[0]):
                e = e_ref[r, row, :]
                v = v_ref[r, row, :]
                even = jnp.where(e == cells, v, even)
                odd = jnp.where(e == cells2, v, odd)
            parts.append(jnp.concatenate([even, odd], axis=1))
        o_ref[:, s * TILE : (s + 1) * TILE] = inverse_tile(jnp.concatenate(parts, axis=0), c_ref)


Z, X, T = 8, 4, 8


def tensor_sum(x):
    x = x + lax.ppermute(x, "tensor", [(t, t ^ 1) for t in range(T)])
    return x + sum(lax.ppermute(x, "tensor", [(t, (t + k) % T) for t in range(T)]) for k in (2, 6, 4))


def shift(x, dz, dx):
    pairs = [(z * X + c, (z + dz) % Z * X + (c + dx) % X) for z in range(Z) for c in range(X)]
    return lax.ppermute(x, "dp", pairs)


def three_of(x):
    return jnp.stack([shift(x, 1, 0), x, shift(x, -1, 0)])


def far_of(three):
    return shift(three, 3, 0), shift(three[:2], -3, 0)


def others_of(eight):
    return [shift(eight, 0, k) for k in (1, 3, 2)]


VMEM_LIMIT = 32 * 1024 * 1024
BIG = 60 * 1024 * 1024


def params(limit=VMEM_LIMIT):
    return pltpu.CompilerParams(vmem_limit_bytes=limit)


def cost(us):
    return pl.CostEstimate(flops=int(us * 1e9), bytes_accessed=int(us * 3.5e6), transcendentals=0)


def whole(shape):
    return pl.BlockSpec(shape, lambda j: (0,) * len(shape))


def shards(momentum, gradient, kept):
    forward, inverse = constants()
    width = momentum.shape[2]
    steps = width // WIDE
    blocks = width // BLK
    per = WIDE // BLK
    band = jnp.arange(KEEP, dtype=jnp.int32) * BAND
    offsets = jnp.transpose(kept[0] - band, (1, 0, 2)).reshape(blocks, 128)
    field_spec = pl.BlockSpec((1, ROWS, WIDE), lambda j: (0, 0, j))
    row_spec = pl.BlockSpec((per, 128), lambda j: (j, 0))
    const_spec = whole((2, 3 * TILE, TILE))
    near = [shift(offsets, 1, 0), shift(offsets, -1, 0)]
    values = pl.pallas_call(
        values_kernel,
        grid=(steps,),
        in_specs=[field_spec, field_spec, row_spec] + [const_spec],
        out_specs=row_spec,
        out_shape=jax.ShapeDtypeStruct((blocks, 128), jnp.float32),
        compiler_params=params(BIG),
        cost_estimate=cost(7),
    )(momentum, gradient, offsets, forward)
    values, *near = lax.optimization_barrier((values, *near))

    def residual_part(first, count, into):
        field = pl.BlockSpec((1, ROWS, WIDE), lambda j: (0, 0, j + first))
        row = pl.BlockSpec((per, 128), lambda j: (j + first, 0))
        more = [] if into is None else [pl.BlockSpec(memory_space=pl.ANY)]
        return pl.pallas_call(
            residual_kernel,
            grid=(count,),
            in_specs=[field, field, row, row, const_spec] + more,
            out_specs=field,
            out_shape=jax.ShapeDtypeStruct(momentum.shape, jnp.float32),
            input_output_aliases={} if into is None else {5: 0},
            compiler_params=params(BIG),
            cost_estimate=cost(4),
        )(momentum, gradient, offsets, values, inverse, *([] if into is None else [into]))

    near_v = [shift(values, 1, 0), shift(values, -1, 0)]
    three = jnp.stack([near[0], offsets, near[1]])
    far = far_of(three)
    residual = residual_part(0, steps // 2, None)
    residual, *near_v = lax.optimization_barrier((residual, *near_v))
    three_v = jnp.stack([near_v[0], values, near_v[1]])
    far_v = far_of(three_v)
    eight = jnp.concatenate([three, *far])
    others = others_of(eight)
    residual = residual_part(steps // 2, steps - steps // 2, residual)
    residual, *far_v = lax.optimization_barrier((residual, *far_v))
    eight_v = jnp.concatenate([three_v, *far_v])
    others_v = others_of(eight_v)
    replicas = 4 * eight.shape[0]
    places, totals, squares = pl.pallas_call(
        merge_kernel,
        out_shape=(
            jax.ShapeDtypeStruct((replicas, blocks, 128), jnp.int32),
            jax.ShapeDtypeStruct((replicas, blocks, 128), jnp.float32),
            jax.ShapeDtypeStruct((8, 128), jnp.float32),
        ),
        compiler_params=params(),
        cost_estimate=cost(3),
    )(eight, *others, eight_v, *others_v)
    whole_spec = whole(places.shape)
    combined = pl.pallas_call(
        combined_kernel,
        grid=(steps,),
        in_specs=[whole_spec, whole_spec, const_spec],
        out_specs=pl.BlockSpec((ROWS, WIDE), lambda j: (0, j)),
        out_shape=jax.ShapeDtypeStruct((ROWS, width), jnp.float32),
        compiler_params=params(),
        cost_estimate=cost(10),
    )(places, totals, inverse)
    total = tensor_sum(squares)
    combined, total = lax.optimization_barrier((combined, total))
    update = combined * lax.rsqrt(jnp.sum(total) / (ROWS * FF) + epsilon)
    return (update, residual)


def solution(mesh):
    return jax.shard_map(
        shards,
        mesh=mesh,
        in_specs=(P("dp", None, "tensor"), P("dp", None, "tensor"), P("dp", None, "tensor", None)),
        out_specs=(P(None, "tensor"), P("dp", None, "tensor")),
        check_vma=False,
    )
```

```python
import functools

import jax
import jax.numpy as jnp
import numpy as np
from jax import lax
from jax.experimental import pallas as pl
from jax.experimental.pallas import tpu as pltpu
from jax.sharding import PartitionSpec as P

FF = 28672
ROWS = 256
BLK = 64
KEEP = 32
BAND = BLK * BLK // KEEP
TILE = 256
WIDE = 1792

decay_rate = 0.9
epsilon = 1e-06


def thirds_np(x):
    high = x.astype(jnp.bfloat16)
    low = (x - high.astype(np.float32)).astype(jnp.bfloat16)
    return np.concatenate([high, low, high])


def constants():
    k = np.arange(BLK)[:, None]
    n = np.arange(BLK)[None, :]
    c = np.cos(np.pi * (2.0 * n + 1.0) * k / (2.0 * BLK)) * np.sqrt(2.0 / BLK)
    c[0] *= 1.0 / np.sqrt(2.0)
    right = np.kron(np.eye(4), c).astype(np.float32)
    order = [p * BLK + 2 * i + h for h in range(2) for p in range(4) for i in range(KEEP)]
    left = right[order]
    forward = np.stack([thirds_np(right.T), thirds_np(left.T)])
    inverse = np.stack([thirds_np(left), thirds_np(right)])
    return forward, inverse


def dot3(x, thirds):
    high = x.astype(jnp.bfloat16)
    low = (x - high.astype(jnp.float32)).astype(jnp.bfloat16)
    return jnp.dot(jnp.concatenate([high, high, low], axis=1), thirds, preferred_element_type=jnp.float32)


def tile(i):
    return slice(i * TILE, (i + 1) * TILE)


def block(q):
    return slice(q * BLK, (q + 1) * BLK)


def field(m_ref, g_ref, i):
    return decay_rate * m_ref[0, :, tile(i)] + g_ref[0, :, tile(i)].astype(jnp.float32)


def both_sides(x, c_ref):
    return dot3(dot3(x, c_ref[0]).T, c_ref[1])


def cells_of():
    cells = lax.broadcasted_iota(jnp.int32, (BLK, 128), 0).astype(jnp.float32)
    return cells, cells + float(BLK)


def values_kernel(m_ref, g_ref, e_ref, c_ref, p_ref):
    first = pl.program_id(0) * (WIDE // BLK)
    cells = cells_of()
    for i in range(WIDE // TILE):
        coeffs = both_sides(field(m_ref, g_ref, i), c_ref)
        for q in range(4):
            row = pl.ds(first + i * 4 + q, 1)
            e = e_ref[row, :]
            own = coeffs[block(q)]
            chosen = jnp.where(e == cells[0], own[:, :128], 0.0) + jnp.where(e == cells[1], own[:, 128:], 0.0)
            p_ref[0, row, :] = e
            p_ref[1, row, :] = jnp.sum(chosen, axis=0, keepdims=True)


def residual_kernel(m_ref, g_ref, p_ref, c_ref, o_ref):
    first = pl.program_id(0) * (WIDE // BLK)
    cells = cells_of()
    for i in range(WIDE // TILE):
        parts = []
        for q in range(4):
            row = pl.ds(first + i * 4 + q, 1)
            e, v = p_ref[0, row, :], p_ref[1, row, :]
            parts.append(jnp.concatenate([jnp.where(e == cell, v, 0.0) for cell in cells], axis=1))
        sent = both_sides(jnp.concatenate(parts, axis=0), c_ref)
        o_ref[0, :, tile(i)] = field(m_ref, g_ref, i) - sent


def merge_kernel(*refs, late):
    *parts, p_ref, sq_ref = refs
    held = replicas_of(parts)

    def rows(g, squares):
        at = pl.ds(pl.multiple_of(g * 8, 8), 8)
        places = [ref[r, 0, at, :] for ref, r in held]
        values = [ref[r, 1, at, :] for ref, r in held]
        for i in range(len(held)):
            place, total = places[i], values[i]
            for j in range(i + 1, len(held)):
                if j == late:
                    p_ref[i, 0, at, :] = place
                    p_ref[i, 1, at, :] = total
                same = place == places[j]
                total = total + jnp.where(same, values[j], 0.0)
                places[j] = jnp.where(same, -1.0 - j, places[j])
            squares = squares + jnp.where(place >= 0.0, total * total, 0.0)
        return squares

    sq_ref[...] = lax.fori_loop(0, p_ref.shape[2] // 8, rows, jnp.zeros((8, 128), jnp.float32))


def replicas_of(parts):
    return [(ref, r) for ref in parts for r in range(ref.shape[0])]


def summed_row(held, row, cell, distinct):
    total = jnp.zeros((BLK, 128), jnp.float32)
    for ref, r in held:
        here = ref[r, 0, row, :] == cell
        value = ref[r, 1, row, :]
        total = jnp.where(here, value, total) if distinct else total + jnp.where(here, value, 0.0)
    return total


def early_kernel(*refs):
    *parts, s_ref = refs
    held = replicas_of(parts)
    first = pl.program_id(0) * (WIDE // BLK)
    cells = cells_of()

    @pl.loop(0, WIDE // BLK)
    def _(q):
        rows = pl.ds(pl.multiple_of(q * BLK, BLK), BLK)
        for half in range(2):
            s_ref[rows, half * 128 : half * 128 + 128] = summed_row(held, pl.ds(first + q, 1), cells[half], False)


def late_kernel(p_ref, before_ref, c_ref, o_ref):
    held = replicas_of([p_ref])
    first = pl.program_id(0) * (WIDE // BLK)
    cells = cells_of()
    for i in range(WIDE // TILE):
        parts = []
        for q in range(4):
            row = pl.ds(first + i * 4 + q, 1)
            parts.append(jnp.concatenate([summed_row(held, row, cell, True) for cell in cells], axis=1))
        summed = before_ref[tile(i), :] + jnp.concatenate(parts, axis=0)
        o_ref[:, tile(i)] = both_sides(summed, c_ref)


def scale_kernel(x_ref, total_ref, o_ref):
    mean = jnp.sum(total_ref[...], keepdims=True) / (ROWS * FF)
    o_ref[...] = x_ref[...] * lax.rsqrt(mean + epsilon)


Z, X, T = 8, 4, 8


def tensor_sum(x):
    x = x + lax.ppermute(x, "tensor", [(t, t ^ 1) for t in range(T)])
    return x + sum(lax.ppermute(x, "tensor", [(t, (t + k) % T) for t in range(T)]) for k in (2, 6, 4))


def shift(x, dz, dx):
    pairs = [(z * X + c, (z + dz) % Z * X + (c + dx) % X) for z in range(Z) for c in range(X)]
    return lax.ppermute(x, "dp", pairs)


VMEM_LIMIT = 32 * 1024 * 1024
MIDDLE = 44 * 1024 * 1024
BIG = 60 * 1024 * 1024


def params(limit=VMEM_LIMIT):
    return pltpu.CompilerParams(vmem_limit_bytes=limit)


def cost(us):
    return pl.CostEstimate(flops=int(us * 1e9), bytes_accessed=int(us * 3.5e6), transcendentals=0)


def whole(shape):
    return pl.BlockSpec(shape, lambda j: (0,) * len(shape))


def across(x):
    return [shift(x, 0, k) for k in (1, 3, 2)]


def shards(momentum, gradient, kept):
    forward, inverse = constants()
    width = momentum.shape[2]
    steps = width // WIDE
    blocks = width // BLK
    band = jnp.arange(KEEP, dtype=jnp.int32) * BAND
    offsets = jnp.transpose(kept[0] - band, (1, 0, 2)).reshape(blocks, 128).astype(jnp.float32)
    field_spec = pl.BlockSpec((1, ROWS, WIDE), lambda j: (0, 0, j))
    const_spec = whole(forward.shape)
    packet_spec = whole((2, blocks, 128))
    packet = pl.pallas_call(
        values_kernel,
        grid=(steps,),
        in_specs=[field_spec, field_spec, whole((blocks, 128)), const_spec],
        out_specs=packet_spec,
        out_shape=jax.ShapeDtypeStruct((2, blocks, 128), jnp.float32),
        compiler_params=params(BIG),
        cost_estimate=cost(8),
    )(momentum, gradient, offsets, forward)
    three = jnp.stack([shift(packet, 1, 0), packet, shift(packet, -1, 0)])
    far = [shift(three, 3, 0), shift(three[:2], -3, 0)]
    three_x = across(three)
    packet, three = lax.optimization_barrier((packet, three))
    residual = pl.pallas_call(
        residual_kernel,
        grid=(steps,),
        in_specs=[field_spec, field_spec, packet_spec, const_spec],
        out_specs=field_spec,
        out_shape=jax.ShapeDtypeStruct(momentum.shape, jnp.float32),
        compiler_params=params(MIDDLE),
        cost_estimate=cost(8),
    )(momentum, gradient, packet, inverse)
    residual, *far = lax.optimization_barrier((residual, *far))
    five = jnp.concatenate(far)
    five_x = across(five)
    sum_spec = pl.BlockSpec((WIDE, TILE), lambda j: (j, 0))
    early = [three, *three_x, five]
    summed = pl.pallas_call(
        early_kernel,
        grid=(steps,),
        in_specs=[whole(x.shape) for x in early],
        out_specs=sum_spec,
        out_shape=jax.ShapeDtypeStruct((width, TILE), jnp.float32),
        compiler_params=params(),
        cost_estimate=cost(7),
    )(*early)
    summed, *five_x = lax.optimization_barrier((summed, *five_x))
    late = sum(x.shape[0] for x in five_x)
    merged, squares = pl.pallas_call(
        functools.partial(merge_kernel, late=late),
        out_shape=(
            jax.ShapeDtypeStruct((late, 2, blocks, 128), jnp.float32),
            jax.ShapeDtypeStruct((8, 128), jnp.float32),
        ),
        compiler_params=params(),
        cost_estimate=cost(2),
    )(*five_x, *early)
    total = tensor_sum(squares)
    combined = pl.pallas_call(
        late_kernel,
        grid=(steps,),
        in_specs=[whole(merged.shape), sum_spec, const_spec],
        out_specs=pl.BlockSpec((ROWS, WIDE), lambda j: (0, j)),
        out_shape=jax.ShapeDtypeStruct((ROWS, width), jnp.float32),
        compiler_params=params(),
        cost_estimate=cost(9),
    )(merged, summed, inverse)
    combined, total = lax.optimization_barrier((combined, total))
    scale_spec = pl.BlockSpec((64, width), lambda j: (j, 0))
    update = pl.pallas_call(
        scale_kernel,
        grid=(ROWS // 64,),
        in_specs=[scale_spec, whole((8, 128))],
        out_specs=scale_spec,
        out_shape=jax.ShapeDtypeStruct((ROWS, width), jnp.float32),
        compiler_params=params(),
        cost_estimate=cost(2),
    )(combined, total)
    return (update, residual)


def solution(mesh):
    return jax.shard_map(
        shards,
        mesh=mesh,
        in_specs=(P("dp", None, "tensor"), P("dp", None, "tensor"), P("dp", None, "tensor", None)),
        out_specs=(P(None, "tensor"), P("dp", None, "tensor")),
        check_vma=False,
    )
```

```python
import functools

import jax
import jax.numpy as jnp
import numpy as np
from jax import lax
from jax.experimental import pallas as pl
from jax.experimental.pallas import tpu as pltpu
from jax.sharding import PartitionSpec as P

FF = 28672
ROWS = 256
BLK = 64
KEEP = 32
BAND = BLK * BLK // KEEP
TILE = 256
WIDE = 1792

decay_rate = 0.9
epsilon = 1e-06


def thirds_np(x):
    high = x.astype(jnp.bfloat16)
    low = (x - high.astype(np.float32)).astype(jnp.bfloat16)
    return np.concatenate([high, low, high])


def constants():
    k = np.arange(BLK)[:, None]
    n = np.arange(BLK)[None, :]
    c = np.cos(np.pi * (2.0 * n + 1.0) * k / (2.0 * BLK)) * np.sqrt(2.0 / BLK)
    c[0] *= 1.0 / np.sqrt(2.0)
    right = np.kron(np.eye(4), c).astype(np.float32)
    order = [p * BLK + 2 * i + h for h in range(2) for p in range(4) for i in range(KEEP)]
    left = right[order]
    forward = np.stack([thirds_np(right.T), thirds_np(left.T)])
    inverse = np.stack([thirds_np(left), thirds_np(right)])
    return forward, inverse


def dot3(x, thirds):
    high = x.astype(jnp.bfloat16)
    low = (x - high.astype(jnp.float32)).astype(jnp.bfloat16)
    return jnp.dot(jnp.concatenate([high, high, low], axis=1), thirds, preferred_element_type=jnp.float32)


def tile(i):
    return slice(i * TILE, (i + 1) * TILE)


def block(q):
    return slice(q * BLK, (q + 1) * BLK)


def field(m_ref, g_ref, i):
    return decay_rate * m_ref[0, :, tile(i)] + g_ref[0, :, tile(i)].astype(jnp.float32)


def both_sides(x, c_ref):
    return dot3(dot3(x, c_ref[0]).T, c_ref[1])


def cells_of():
    cells = lax.broadcasted_iota(jnp.int32, (BLK, 128), 0).astype(jnp.float32)
    return cells, cells + float(BLK)


def values_kernel(m_ref, g_ref, k_ref, c_ref, p_ref):
    first = pl.program_id(0) * (WIDE // BLK)
    cells = cells_of()

    @pl.when(pl.program_id(0) == 0)
    def _():
        band = lax.broadcasted_iota(jnp.int32, k_ref.shape, 0) % KEEP
        p_ref[0] = (k_ref[...] - band * BAND).astype(jnp.float32).T

    for i in range(WIDE // TILE):
        coeffs = both_sides(field(m_ref, g_ref, i), c_ref)
        for q in range(4):
            row = pl.ds(first + i * 4 + q, 1)
            e = p_ref[0, row, :]
            own = coeffs[block(q)]
            chosen = jnp.where(e == cells[0], own[:, :128], 0.0) + jnp.where(e == cells[1], own[:, 128:], 0.0)
            p_ref[1, row, :] = jnp.sum(chosen, axis=0, keepdims=True)


def residual_kernel(m_ref, g_ref, p_ref, c_ref, o_ref):
    first = pl.program_id(0) * (WIDE // BLK)
    cells = cells_of()
    for i in range(WIDE // TILE):
        parts = []
        for q in range(4):
            row = pl.ds(first + i * 4 + q, 1)
            e, v = p_ref[0, row, :], p_ref[1, row, :]
            parts.append(jnp.concatenate([jnp.where(e == cell, v, 0.0) for cell in cells], axis=1))
        sent = both_sides(jnp.concatenate(parts, axis=0), c_ref)
        o_ref[0, :, tile(i)] = field(m_ref, g_ref, i) - sent


def merge_kernel(*refs, groups, distinct, merged, squared):
    outs = refs[sum(groups) :]
    held, bounds = [], [0]
    for count in groups:
        start = len(bounds) - 1 and sum(groups[: len(bounds) - 1])
        held += replicas_of(refs[start : start + count])
        bounds.append(len(held))
    group_of = [g for g in range(len(groups)) for _ in range(bounds[g], bounds[g + 1])]

    def rows(step, squares):
        at = pl.ds(pl.multiple_of(step * 8, 8), 8)
        places = [ref[r, 0, at, :] for ref, r in held]
        values = [ref[r, 1, at, :] for ref, r in held]
        for i in range(len(held)):
            place, total, group = places[i], values[i], group_of[i]
            for j in range(i + 1, len(held) + 1):
                if j == bounds[group + 1] and group < merged:
                    outs[group][i - bounds[group], 0, at, :] = place
                    outs[group][i - bounds[group], 1, at, :] = total
                if j == len(held) or (not squared and group_of[j] != group):
                    break
                if distinct and group == len(groups) - 1:
                    break
                same = place == places[j]
                total = total + jnp.where(same, values[j], 0.0)
                places[j] = jnp.where(same, -1.0 - j, places[j])
            if squared:
                squares = squares + jnp.where(place >= 0.0, total * total, 0.0)
        return squares

    squares = lax.fori_loop(0, refs[0].shape[2] // 8, rows, jnp.zeros((8, 128), jnp.float32))
    if squared:
        outs[-1][...] = squares


def replicas_of(parts):
    return [(ref, r) for ref in parts for r in range(ref.shape[0])]


def summed_row(held, row, cell, distinct):
    total = jnp.zeros((BLK, 128), jnp.float32)
    for ref, r in held:
        here = ref[r, 0, row, :] == cell
        value = ref[r, 1, row, :]
        total = jnp.where(here, value, total) if distinct else total + jnp.where(here, value, 0.0)
    return total


def add_kernel(*refs, distinct, before):
    *parts, s_ref = refs
    before_ref = parts.pop() if before else None
    held = replicas_of(parts)
    first = pl.program_id(0) * (WIDE // BLK)
    cells = cells_of()

    @pl.loop(0, WIDE // BLK)
    def _(q):
        rows = pl.ds(pl.multiple_of(q * BLK, BLK), BLK)
        for half in range(2):
            lanes = slice(half * 128, half * 128 + 128)
            total = summed_row(held, pl.ds(first + q, 1), cells[half], distinct)
            s_ref[rows, lanes] = total + before_ref[rows, lanes] if before else total


def late_tiles(p_ref, before_ref, c_ref, o_ref, first, scale):
    held = replicas_of([p_ref])
    cells = cells_of()
    for i in range(WIDE // TILE):
        parts = []
        for q in range(4):
            row = slice(first + i * 4 + q, first + i * 4 + q + 1)
            parts.append(jnp.concatenate([summed_row(held, row, cell, True) for cell in cells], axis=1))
        summed = before_ref[tile(i), :] + jnp.concatenate(parts, axis=0)
        out = both_sides(summed, c_ref)
        o_ref[:, tile(i)] = out if scale is None else out * scale


def left_kernel(p_ref, before_ref, c_ref, o_ref):
    late_tiles(p_ref, before_ref, c_ref, o_ref, 0, None)


def right_kernel(p_ref, before_ref, c_ref, x_ref, total_ref, o_ref):
    mean = jnp.sum(total_ref[...], keepdims=True) / (ROWS * FF)
    scale = lax.rsqrt(mean + epsilon)

    @pl.when(pl.program_id(0) == 0)
    def _():
        late_tiles(p_ref, before_ref, c_ref, o_ref, WIDE // BLK, scale)

    @pl.when(pl.program_id(0) == 1)
    def _():
        o_ref[...] = x_ref[...] * scale


Z, X, T = 8, 4, 8


def tensor_sum(x):
    x = x + lax.ppermute(x, "tensor", [(t, t ^ 1) for t in range(T)])
    return x + sum(lax.ppermute(x, "tensor", [(t, (t + k) % T) for t in range(T)]) for k in (2, 6, 4))


def shift(x, dz, dx):
    pairs = [(z * X + c, (z + dz) % Z * X + (c + dx) % X) for z in range(Z) for c in range(X)]
    return lax.ppermute(x, "dp", pairs)


VMEM_LIMIT = 32 * 1024 * 1024
MIDDLE = 59 * 1024 * 1024
BIG = 60 * 1024 * 1024


def params(limit=VMEM_LIMIT):
    return pltpu.CompilerParams(vmem_limit_bytes=limit)


def cost(us):
    return pl.CostEstimate(flops=int(us * 1e9), bytes_accessed=int(us * 3.5e6), transcendentals=0)


def whole(shape):
    return pl.BlockSpec(shape, lambda j: (0,) * len(shape))


def across(x):
    return [shift(x, 0, k) for k in (1, 3, 2)]


def shards(momentum, gradient, kept):
    forward, inverse = constants()
    width = momentum.shape[2]
    steps = width // WIDE
    blocks = width // BLK
    field_spec = pl.BlockSpec((1, ROWS, WIDE), lambda j: (0, 0, j))
    const_spec = whole(forward.shape)
    places = jnp.transpose(kept[0], (0, 2, 1)).reshape(ROWS // BLK * KEEP, blocks)
    packet_spec = whole((2, blocks, 128))
    packet = pl.pallas_call(
        values_kernel,
        grid=(steps,),
        in_specs=[field_spec, field_spec, whole(places.shape), const_spec],
        out_specs=packet_spec,
        out_shape=jax.ShapeDtypeStruct((2, blocks, 128), jnp.float32),
        compiler_params=params(BIG),
        cost_estimate=cost(8),
    )(momentum, gradient, places, forward)
    three = jnp.stack([shift(packet, 1, 0), packet, shift(packet, -1, 0)])
    far = [shift(three, 3, 0), shift(three, -3, 0)]
    three_x = across(three)
    packet, three = lax.optimization_barrier((packet, three))
    residual = pl.pallas_call(
        residual_kernel,
        grid=(steps,),
        in_specs=[field_spec, field_spec, packet_spec, const_spec],
        out_specs=field_spec,
        out_shape=jax.ShapeDtypeStruct(momentum.shape, jnp.float32),
        compiler_params=params(MIDDLE),
        cost_estimate=cost(8),
    )(momentum, gradient, packet, inverse)
    residual, *far = lax.optimization_barrier((residual, *far))
    five = jnp.concatenate([far[0], far[1][:2]])
    five_x = across(five)
    sum_spec = pl.BlockSpec((WIDE, TILE), lambda j: (j, 0))
    early = [three, *three_x, five]

    def merge_call(groups, us, **flags):
        parts = [x for group in groups for x in group]
        shapes = [
            jax.ShapeDtypeStruct((sum(x.shape[0] for x in group), 2, blocks, 128), jnp.float32)
            for group in groups[: flags["merged"]]
        ]
        if flags["squared"]:
            shapes.append(jax.ShapeDtypeStruct((8, 128), jnp.float32))
        return pl.pallas_call(
            functools.partial(merge_kernel, groups=[len(group) for group in groups], **flags),
            out_shape=shapes,
            compiler_params=params(),
            cost_estimate=cost(us),
        )(*parts)

    def add_call(parts, before, distinct, us):
        return pl.pallas_call(
            functools.partial(add_kernel, distinct=distinct, before=len(before) > 0),
            grid=(steps,),
            in_specs=[whole(x.shape) for x in parts] + [sum_spec] * len(before),
            out_specs=sum_spec,
            out_shape=jax.ShapeDtypeStruct((width, TILE), jnp.float32),
            input_output_aliases={len(parts): 0} if before else {},
            compiler_params=params(),
            cost_estimate=cost(us),
        )(*parts, *before)

    (early_merged,) = merge_call([early], 1, distinct=False, merged=1, squared=False)
    summed = add_call([early_merged], [], True, 5)
    summed, *five_x = lax.optimization_barrier((summed, *five_x))
    merged, squares = merge_call([five_x, [early_merged]], 2, distinct=True, merged=1, squared=True)
    total = tensor_sum(squares)
    half_shape = jax.ShapeDtypeStruct((ROWS, WIDE), jnp.float32)
    half_spec = whole(half_shape.shape)
    combined = pl.pallas_call(
        left_kernel,
        grid=(1,),
        in_specs=[whole(merged.shape), pl.BlockSpec((WIDE, TILE), lambda j: (0, 0)), const_spec],
        out_specs=half_spec,
        out_shape=half_shape,
        compiler_params=params(),
        cost_estimate=cost(4),
    )(merged, summed, inverse)
    combined, total = lax.optimization_barrier((combined, total))
    update = pl.pallas_call(
        right_kernel,
        grid=(2,),
        in_specs=[whole(merged.shape), pl.BlockSpec((WIDE, TILE), lambda j: (1, 0)), const_spec, half_spec, whole((8, 128))],
        out_specs=pl.BlockSpec((ROWS, WIDE), lambda j: (0, 1 - j)),
        out_shape=jax.ShapeDtypeStruct((ROWS, width), jnp.float32),
        compiler_params=params(),
        cost_estimate=cost(5),
    )(merged, summed, inverse, combined, total)
    return (update, residual)


def solution(mesh):
    return jax.shard_map(
        shards,
        mesh=mesh,
        in_specs=(P("dp", None, "tensor"), P("dp", None, "tensor"), P("dp", None, "tensor", None)),
        out_specs=(P(None, "tensor"), P("dp", None, "tensor")),
        check_vma=False,
    )
```

```python
import functools

import jax
import jax.numpy as jnp
import numpy as np
from jax import lax
from jax.experimental import pallas as pl
from jax.experimental.pallas import tpu as pltpu
from jax.sharding import PartitionSpec as P

FF = 28672
ROWS = 256
BLK = 64
KEEP = 32
BAND = BLK * BLK // KEEP
TILE = 256
WIDE = 1792

decay_rate = 0.9
epsilon = 1e-06


def thirds_np(x):
    high = x.astype(jnp.bfloat16)
    low = (x - high.astype(np.float32)).astype(jnp.bfloat16)
    return np.concatenate([high, low, high])


def constants():
    k = np.arange(BLK)[:, None]
    n = np.arange(BLK)[None, :]
    c = np.cos(np.pi * (2.0 * n + 1.0) * k / (2.0 * BLK)) * np.sqrt(2.0 / BLK)
    c[0] *= 1.0 / np.sqrt(2.0)
    right = np.kron(np.eye(4), c).astype(np.float32)
    order = [p * BLK + 2 * i + h for h in range(2) for p in range(4) for i in range(KEEP)]
    left = right[order]
    forward = np.stack([thirds_np(right.T), thirds_np(left.T)])
    inverse = np.stack([thirds_np(left), thirds_np(right)])
    return forward, inverse


def dot3(x, thirds):
    high = x.astype(jnp.bfloat16)
    low = (x - high.astype(jnp.float32)).astype(jnp.bfloat16)
    return jnp.dot(jnp.concatenate([high, high, low], axis=1), thirds, preferred_element_type=jnp.float32)


def tile(i):
    return slice(i * TILE, (i + 1) * TILE)


def block(q):
    return slice(q * BLK, (q + 1) * BLK)


def field(m_ref, g_ref, i):
    return decay_rate * m_ref[0, :, tile(i)] + g_ref[0, :, tile(i)].astype(jnp.float32)


def both_sides(x, c_ref):
    return dot3(dot3(x, c_ref[0]).T, c_ref[1])


def cells_of():
    cells = lax.broadcasted_iota(jnp.int32, (BLK, 128), 0).astype(jnp.float32)
    return cells, cells + float(BLK)


def values_kernel(m_ref, g_ref, k_ref, c_ref, p_ref):
    first = pl.program_id(0) * (WIDE // BLK)
    cells = cells_of()

    @pl.when(pl.program_id(0) == 0)
    def _():
        band = lax.broadcasted_iota(jnp.int32, k_ref.shape, 0) % KEEP
        p_ref[0] = (k_ref[...] - band * BAND).astype(jnp.float32).T

    for i in range(WIDE // TILE):
        coeffs = both_sides(field(m_ref, g_ref, i), c_ref)
        for q in range(4):
            row = pl.ds(first + i * 4 + q, 1)
            e = p_ref[0, row, :]
            own = coeffs[block(q)]
            chosen = jnp.where(e == cells[0], own[:, :128], 0.0) + jnp.where(e == cells[1], own[:, 128:], 0.0)
            p_ref[1, row, :] = jnp.sum(chosen, axis=0, keepdims=True)


def residual_kernel(m_ref, g_ref, p_ref, c_ref, *rest, first):
    o_ref = rest[-1]
    cells = cells_of()
    for i in range(WIDE // TILE):
        parts = []
        for q in range(4):
            row = slice(first + i * 4 + q, first + i * 4 + q + 1)
            e, v = p_ref[0, row, :], p_ref[1, row, :]
            parts.append(jnp.concatenate([jnp.where(e == cell, v, 0.0) for cell in cells], axis=1))
        sent = both_sides(jnp.concatenate(parts, axis=0), c_ref)
        o_ref[0, :, tile(i)] = field(m_ref, g_ref, i) - sent


def merge_kernel(*refs, groups, distinct, merged, squared):
    outs = refs[sum(groups) :]
    held, bounds = [], [0]
    for count in groups:
        start = len(bounds) - 1 and sum(groups[: len(bounds) - 1])
        held += replicas_of(refs[start : start + count])
        bounds.append(len(held))
    group_of = [g for g in range(len(groups)) for _ in range(bounds[g], bounds[g + 1])]

    def rows(step, squares):
        at = pl.ds(pl.multiple_of(step * 8, 8), 8)
        places = [ref[r, 0, at, :] for ref, r in held]
        values = [ref[r, 1, at, :] for ref, r in held]
        for i in range(len(held)):
            place, total, group = places[i], values[i], group_of[i]
            for j in range(i + 1, len(held) + 1):
                if j == bounds[group + 1] and group < merged:
                    outs[group][i - bounds[group], 0, at, :] = place
                    outs[group][i - bounds[group], 1, at, :] = total
                if j == len(held) or (not squared and group_of[j] != group):
                    break
                if distinct and group == len(groups) - 1:
                    break
                same = place == places[j]
                total = total + jnp.where(same, values[j], 0.0)
                places[j] = jnp.where(same, -1.0 - j, places[j])
            if squared:
                squares = squares + jnp.where(place >= 0.0, total * total, 0.0)
        return squares

    squares = lax.fori_loop(0, refs[0].shape[2] // 8, rows, jnp.zeros((8, 128), jnp.float32))
    if squared:
        outs[-1][...] = squares


def replicas_of(parts):
    return [(ref, r) for ref in parts for r in range(ref.shape[0])]


def chosen_row(held, row):
    cells = [cell.astype(jnp.bfloat16) for cell in cells_of()]
    high = [jnp.zeros((BLK, 128), jnp.bfloat16)] * 2
    low = list(high)
    for ref, r in held:
        place = jnp.broadcast_to(ref[r, 0, row, :], (16, 128)).astype(jnp.bfloat16)
        value = jnp.broadcast_to(ref[r, 1, row, :], (16, 128))
        top = value.astype(jnp.bfloat16)
        rest = (value - top.astype(jnp.float32)).astype(jnp.bfloat16)
        place, top, rest = (jnp.concatenate([x] * (BLK // 16), axis=0) for x in (place, top, rest))
        for half in range(2):
            here = place == cells[half]
            high[half] = jnp.where(here, top, high[half])
            low[half] = jnp.where(here, rest, low[half])
    return jnp.concatenate(high, axis=1).astype(jnp.float32) + jnp.concatenate(low, axis=1).astype(jnp.float32)


def add_kernel(*refs):
    *parts, s_ref = refs
    held = replicas_of(parts)
    first = pl.program_id(0) * (WIDE // BLK)

    @pl.loop(0, WIDE // BLK)
    def _(q):
        s_ref[pl.ds(pl.multiple_of(q * BLK, BLK), BLK), :] = chosen_row(held, pl.ds(first + q, 1))


def late_tiles(p_ref, before_ref, c_ref, o_ref, first, scale):
    held = replicas_of([p_ref])
    for i in range(WIDE // TILE):
        parts = []
        for q in range(4):
            row = slice(first + i * 4 + q, first + i * 4 + q + 1)
            parts.append(chosen_row(held, row))
        summed = before_ref[tile(i), :] + jnp.concatenate(parts, axis=0)
        out = both_sides(summed, c_ref)
        o_ref[:, tile(i)] = out if scale is None else out * scale


def left_kernel(p_ref, before_ref, c_ref, o_ref):
    late_tiles(p_ref, before_ref, c_ref, o_ref, 0, None)


def right_kernel(p_ref, before_ref, c_ref, x_ref, total_ref, o_ref):
    mean = jnp.sum(total_ref[...], keepdims=True) / (ROWS * FF)
    scale = lax.rsqrt(mean + epsilon)

    @pl.when(pl.program_id(0) == 0)
    def _():
        late_tiles(p_ref, before_ref, c_ref, o_ref, WIDE // BLK, scale)

    @pl.when(pl.program_id(0) == 1)
    def _():
        o_ref[...] = x_ref[...] * scale


Z, X, T = 8, 4, 8


def tensor_sum(x):
    x = x + lax.ppermute(x, "tensor", [(t, t ^ 1) for t in range(T)])
    return x + sum(lax.ppermute(x, "tensor", [(t, (t + k) % T) for t in range(T)]) for k in (2, 6, 4))


def shift(x, dz, dx):
    pairs = [(z * X + c, (z + dz) % Z * X + (c + dx) % X) for z in range(Z) for c in range(X)]
    return lax.ppermute(x, "dp", pairs)


VMEM_LIMIT = 32 * 1024 * 1024
SMALLER = 55 * 1024 * 1024
MIDDLE = 59 * 1024 * 1024
BIG = 60 * 1024 * 1024


def params(limit=VMEM_LIMIT):
    return pltpu.CompilerParams(vmem_limit_bytes=limit)


def cost(us):
    return pl.CostEstimate(flops=int(us * 1e9), bytes_accessed=int(us * 3.5e6), transcendentals=0)


def whole(shape):
    return pl.BlockSpec(shape, lambda j: (0,) * len(shape))


def across(x):
    return [shift(x, 0, k) for k in (1, 3, 2)]


def shards(momentum, gradient, kept):
    forward, inverse = constants()
    width = momentum.shape[2]
    steps = width // WIDE
    blocks = width // BLK
    field_spec = pl.BlockSpec((1, ROWS, WIDE), lambda j: (0, 0, j))
    const_spec = whole(forward.shape)
    places = jnp.transpose(kept[0], (0, 2, 1)).reshape(ROWS // BLK * KEEP, blocks)
    packet_spec = whole((2, blocks, 128))
    packet = pl.pallas_call(
        values_kernel,
        grid=(steps,),
        in_specs=[field_spec, field_spec, whole(places.shape), const_spec],
        out_specs=packet_spec,
        out_shape=jax.ShapeDtypeStruct((2, blocks, 128), jnp.float32),
        compiler_params=params(BIG),
        cost_estimate=cost(8),
    )(momentum, gradient, places, forward)
    opposite = lax.optimization_barrier(-packet)
    three = jnp.stack([shift(packet, 1, 0), -opposite, shift(packet, -1, 0)])
    far = [shift(three, 3, 0), shift(three, -3, 0)]
    three_x = across(three)
    packet, three = lax.optimization_barrier((packet, three))

    def residual_part(part, into):
        half = pl.BlockSpec((1, ROWS, WIDE), lambda j: (0, 0, part))
        return pl.pallas_call(
            functools.partial(residual_kernel, first=part * (WIDE // BLK)),
            grid=(1,),
            in_specs=[half, half, packet_spec, const_spec] + [pl.BlockSpec(memory_space=pl.ANY)] * len(into),
            out_specs=half,
            out_shape=jax.ShapeDtypeStruct(momentum.shape, jnp.float32),
            input_output_aliases={4: 0} if into else {},
            compiler_params=params(SMALLER if into else MIDDLE),
            cost_estimate=cost(4),
        )(momentum, gradient, packet, inverse, *into)

    residual = residual_part(0, [])
    residual, *far = lax.optimization_barrier((residual, *far))
    five = jnp.concatenate([far[0], far[1][:2]])
    five_x = across(five)
    sum_spec = pl.BlockSpec((WIDE, TILE), lambda j: (j, 0))
    early = [three, *three_x, five]

    def merge_call(groups, us, **flags):
        parts = [x for group in groups for x in group]
        shapes = [
            jax.ShapeDtypeStruct((sum(x.shape[0] for x in group), 2, blocks, 128), jnp.float32)
            for group in groups[: flags["merged"]]
        ]
        if flags["squared"]:
            shapes.append(jax.ShapeDtypeStruct((8, 128), jnp.float32))
        return pl.pallas_call(
            functools.partial(merge_kernel, groups=[len(group) for group in groups], **flags),
            out_shape=shapes,
            compiler_params=params(),
            cost_estimate=cost(us),
        )(*parts)

    (early_merged,) = merge_call([early], 1, distinct=False, merged=1, squared=False)
    summed = pl.pallas_call(
        add_kernel,
        grid=(steps,),
        in_specs=[whole(early_merged.shape)],
        out_specs=sum_spec,
        out_shape=jax.ShapeDtypeStruct((width, TILE), jnp.float32),
        compiler_params=params(),
        cost_estimate=cost(5),
    )(early_merged)
    residual, five = lax.optimization_barrier((residual, five))
    residual = residual_part(1, [residual])
    summed, residual, *five_x = lax.optimization_barrier((summed, residual, *five_x))
    merged, squares = merge_call([five_x, [early_merged]], 2, distinct=True, merged=1, squared=True)
    total = tensor_sum(squares)
    half_shape = jax.ShapeDtypeStruct((ROWS, WIDE), jnp.float32)
    half_spec = whole(half_shape.shape)
    combined = pl.pallas_call(
        left_kernel,
        grid=(1,),
        in_specs=[whole(merged.shape), pl.BlockSpec((WIDE, TILE), lambda j: (0, 0)), const_spec],
        out_specs=half_spec,
        out_shape=half_shape,
        compiler_params=params(),
        cost_estimate=cost(4),
    )(merged, summed, inverse)
    combined, total = lax.optimization_barrier((combined, total))
    update = pl.pallas_call(
        right_kernel,
        grid=(2,),
        in_specs=[whole(merged.shape), pl.BlockSpec((WIDE, TILE), lambda j: (1, 0)), const_spec, half_spec, whole((8, 128))],
        out_specs=pl.BlockSpec((ROWS, WIDE), lambda j: (0, 1 - j)),
        out_shape=jax.ShapeDtypeStruct((ROWS, width), jnp.float32),
        compiler_params=params(),
        cost_estimate=cost(5),
    )(merged, summed, inverse, combined, total)
    return (update, residual)


def solution(mesh):
    return jax.shard_map(
        shards,
        mesh=mesh,
        in_specs=(P("dp", None, "tensor"), P("dp", None, "tensor"), P("dp", None, "tensor", None)),
        out_specs=(P(None, "tensor"), P("dp", None, "tensor")),
        check_vma=False,
    )
```

```python
import functools

import jax
import jax.numpy as jnp
import numpy as np
from jax import lax
from jax.experimental import pallas as pl
from jax.experimental.pallas import tpu as pltpu
from jax.sharding import PartitionSpec as P

FF = 28672
ROWS = 256
BLK = 64
KEEP = 32
BAND = BLK * BLK // KEEP
TILE = 256
WIDE = 1792

decay_rate = 0.9
epsilon = 1e-06


def thirds_np(x):
    high = x.astype(jnp.bfloat16)
    low = (x - high.astype(np.float32)).astype(jnp.bfloat16)
    return np.concatenate([high, low, high])


def constants():
    k = np.arange(BLK)[:, None]
    n = np.arange(BLK)[None, :]
    c = np.cos(np.pi * (2.0 * n + 1.0) * k / (2.0 * BLK)) * np.sqrt(2.0 / BLK)
    c[0] *= 1.0 / np.sqrt(2.0)
    right = np.kron(np.eye(4), c).astype(np.float32)
    order = [p * BLK + 2 * i + h for h in range(2) for p in range(4) for i in range(KEEP)]
    left = right[order]
    forward = np.stack([thirds_np(right.T), thirds_np(left.T)])
    inverse = np.stack([thirds_np(left), thirds_np(right)])
    return forward, inverse


def dot3(x, thirds):
    high = x.astype(jnp.bfloat16)
    low = (x - high.astype(jnp.float32)).astype(jnp.bfloat16)
    return jnp.dot(jnp.concatenate([high, high, low], axis=1), thirds, preferred_element_type=jnp.float32)


def tile(i):
    return slice(i * TILE, (i + 1) * TILE)


def block(q):
    return slice(q * BLK, (q + 1) * BLK)


def field(m_ref, g_ref, i):
    return decay_rate * m_ref[0, :, tile(i)] + g_ref[0, :, tile(i)].astype(jnp.float32)


def both_sides(x, c_ref):
    return dot3(dot3(x, c_ref[0]).T, c_ref[1])


def cells_of():
    cells = lax.broadcasted_iota(jnp.int32, (BLK, 128), 0).astype(jnp.float32)
    return cells, cells + float(BLK)


def values_kernel(m_ref, g_ref, k_ref, c_ref, p_ref):
    first = pl.program_id(0) * (WIDE // BLK)
    cells = cells_of()

    @pl.when(pl.program_id(0) == 0)
    def _():
        band = lax.broadcasted_iota(jnp.int32, k_ref.shape, 0) % KEEP
        p_ref[0] = (k_ref[...] - band * BAND).astype(jnp.float32).T

    for i in range(WIDE // TILE):
        coeffs = both_sides(field(m_ref, g_ref, i), c_ref)
        for q in range(4):
            row = pl.ds(first + i * 4 + q, 1)
            e = p_ref[0, row, :]
            own = coeffs[block(q)]
            chosen = jnp.where(e == cells[0], own[:, :128], 0.0) + jnp.where(e == cells[1], own[:, 128:], 0.0)
            p_ref[1, row, :] = jnp.sum(chosen, axis=0, keepdims=True)


def residual_kernel(m_ref, g_ref, p_ref, c_ref, *rest, first):
    o_ref = rest[-1]
    cells = cells_of()
    for i in range(WIDE // TILE):
        parts = []
        for q in range(4):
            row = slice(first + i * 4 + q, first + i * 4 + q + 1)
            e, v = p_ref[0, row, :], p_ref[1, row, :]
            parts.append(jnp.concatenate([jnp.where(e == cell, v, 0.0) for cell in cells], axis=1))
        sent = both_sides(jnp.concatenate(parts, axis=0), c_ref)
        o_ref[0, :, tile(i)] = field(m_ref, g_ref, i) - sent


def merge_kernel(*refs, groups, distinct, merged, squared):
    outs = refs[sum(groups) :]
    held, bounds = [], [0]
    for count in groups:
        start = len(bounds) - 1 and sum(groups[: len(bounds) - 1])
        held += replicas_of(refs[start : start + count])
        bounds.append(len(held))
    group_of = [g for g in range(len(groups)) for _ in range(bounds[g], bounds[g + 1])]

    def rows(step, squares):
        at = pl.ds(pl.multiple_of(step * 8, 8), 8)
        places = [ref[r, 0, at, :] for ref, r in held]
        values = [ref[r, 1, at, :] for ref, r in held]
        for i in range(len(held)):
            place, total, group = places[i], values[i], group_of[i]
            for j in range(i + 1, len(held) + 1):
                if j == bounds[group + 1] and group < merged:
                    outs[group][i - bounds[group], 0, at, :] = place
                    outs[group][i - bounds[group], 1, at, :] = total
                if j == len(held) or (not squared and group_of[j] != group):
                    break
                if distinct and group == len(groups) - 1:
                    break
                same = place == places[j]
                total = total + jnp.where(same, values[j], 0.0)
                places[j] = jnp.where(same, -1.0 - j, places[j])
            if squared:
                squares = squares + jnp.where(place >= 0.0, total * total, 0.0)
        return squares

    squares = lax.fori_loop(0, refs[0].shape[2] // 8, rows, jnp.zeros((8, 128), jnp.float32))
    if squared:
        outs[-1][...] = squares


def replicas_of(parts):
    return [(ref, r) for ref in parts for r in range(ref.shape[0])]


def chosen_row(held, row):
    cells = [cell.astype(jnp.bfloat16) for cell in cells_of()]
    high = [jnp.zeros((BLK, 128), jnp.bfloat16)] * 2
    low = list(high)
    for ref, r in held:
        place = jnp.broadcast_to(ref[r, 0, row, :], (16, 128)).astype(jnp.bfloat16)
        value = jnp.broadcast_to(ref[r, 1, row, :], (16, 128))
        top = value.astype(jnp.bfloat16)
        rest = (value - top.astype(jnp.float32)).astype(jnp.bfloat16)
        place, top, rest = (jnp.concatenate([x] * (BLK // 16), axis=0) for x in (place, top, rest))
        for half in range(2):
            here = place == cells[half]
            high[half] = jnp.where(here, top, high[half])
            low[half] = jnp.where(here, rest, low[half])
    return jnp.concatenate(high, axis=1).astype(jnp.float32) + jnp.concatenate(low, axis=1).astype(jnp.float32)


def add_kernel(*refs):
    *parts, s_ref = refs
    held = replicas_of(parts)
    first = pl.program_id(0) * (WIDE // BLK)

    @pl.loop(0, WIDE // TILE)
    def _(i):
        for u in range(4):
            q = i * 4 + u
            s_ref[pl.ds(pl.multiple_of(q * BLK, BLK), BLK), :] = chosen_row(held, pl.ds(first + q, 1))


def late_tiles(p_ref, before_ref, c_ref, o_ref, first, scale):
    held = replicas_of([p_ref])
    for i in range(WIDE // TILE):
        parts = []
        for q in range(4):
            row = slice(first + i * 4 + q, first + i * 4 + q + 1)
            parts.append(chosen_row(held, row))
        summed = before_ref[tile(i), :] + jnp.concatenate(parts, axis=0)
        out = both_sides(summed, c_ref)
        o_ref[:, tile(i)] = out if scale is None else out * scale


def left_kernel(p_ref, before_ref, c_ref, o_ref):
    late_tiles(p_ref, before_ref, c_ref, o_ref, 0, None)


def right_kernel(p_ref, before_ref, c_ref, x_ref, total_ref, o_ref):
    mean = jnp.sum(total_ref[...], keepdims=True) / (ROWS * FF)
    scale = lax.rsqrt(mean + epsilon)

    @pl.when(pl.program_id(0) == 0)
    def _():
        late_tiles(p_ref, before_ref, c_ref, o_ref, WIDE // BLK, scale)

    @pl.when(pl.program_id(0) == 1)
    def _():
        o_ref[...] = x_ref[...] * scale


Z, X, T = 8, 4, 8


def tensor_sum(x):
    x = x + lax.ppermute(x, "tensor", [(t, t ^ 1) for t in range(T)])
    return x + sum(lax.ppermute(x, "tensor", [(t, (t + k) % T) for t in range(T)]) for k in (2, 6, 4))


def shift(x, dz, dx):
    pairs = [(z * X + c, (z + dz) % Z * X + (c + dx) % X) for z in range(Z) for c in range(X)]
    return lax.ppermute(x, "dp", pairs)


VMEM_LIMIT = 32 * 1024 * 1024
SMALLER = 55 * 1024 * 1024
MIDDLE = 59 * 1024 * 1024
BIG = 60 * 1024 * 1024


def params(limit=VMEM_LIMIT):
    return pltpu.CompilerParams(vmem_limit_bytes=limit)


def cost(us):
    return pl.CostEstimate(flops=int(us * 1e9), bytes_accessed=int(us * 3.5e6), transcendentals=0)


def whole(shape):
    return pl.BlockSpec(shape, lambda j: (0,) * len(shape))


def across(x):
    return [shift(x, 0, k) for k in (1, 3, 2)]


def shards(momentum, gradient, kept):
    forward, inverse = constants()
    width = momentum.shape[2]
    steps = width // WIDE
    blocks = width // BLK
    field_spec = pl.BlockSpec((1, ROWS, WIDE), lambda j: (0, 0, j))
    const_spec = whole(forward.shape)
    places = jnp.transpose(kept[0], (0, 2, 1)).reshape(ROWS // BLK * KEEP, blocks)
    packet_spec = whole((2, blocks, 128))
    packet = pl.pallas_call(
        values_kernel,
        grid=(steps,),
        in_specs=[field_spec, field_spec, whole(places.shape), const_spec],
        out_specs=packet_spec,
        out_shape=jax.ShapeDtypeStruct((2, blocks, 128), jnp.float32),
        compiler_params=params(BIG),
        cost_estimate=cost(8),
    )(momentum, gradient, places, forward)
    opposite = lax.optimization_barrier(-packet)
    three = jnp.stack([shift(packet, 1, 0), -opposite, shift(packet, -1, 0)])
    far = [shift(three, 3, 0), shift(three, -3, 0)]
    three_x = across(three)
    packet, three = lax.optimization_barrier((packet, three))

    def residual_part(part, into):
        half = pl.BlockSpec((1, ROWS, WIDE), lambda j: (0, 0, part))
        return pl.pallas_call(
            functools.partial(residual_kernel, first=part * (WIDE // BLK)),
            grid=(1,),
            in_specs=[half, half, packet_spec, const_spec] + [pl.BlockSpec(memory_space=pl.ANY)] * len(into),
            out_specs=half,
            out_shape=jax.ShapeDtypeStruct(momentum.shape, jnp.float32),
            input_output_aliases={4: 0} if into else {},
            compiler_params=params(SMALLER if into else MIDDLE),
            cost_estimate=cost(4),
        )(momentum, gradient, packet, inverse, *into)

    residual = residual_part(0, [])
    residual, *far = lax.optimization_barrier((residual, *far))
    five = jnp.concatenate([far[0], far[1][:2]])
    five_x = across(five)
    sum_spec = pl.BlockSpec((WIDE, TILE), lambda j: (j, 0))
    early = [three, *three_x, five]

    def merge_call(groups, us, **flags):
        parts = [x for group in groups for x in group]
        shapes = [
            jax.ShapeDtypeStruct((sum(x.shape[0] for x in group), 2, blocks, 128), jnp.float32)
            for group in groups[: flags["merged"]]
        ]
        if flags["squared"]:
            shapes.append(jax.ShapeDtypeStruct((8, 128), jnp.float32))
        return pl.pallas_call(
            functools.partial(merge_kernel, groups=[len(group) for group in groups], **flags),
            out_shape=shapes,
            compiler_params=params(),
            cost_estimate=cost(us),
        )(*parts)

    (early_merged,) = merge_call([early], 1, distinct=False, merged=1, squared=False)
    summed = pl.pallas_call(
        add_kernel,
        grid=(steps,),
        in_specs=[whole(early_merged.shape)],
        out_specs=sum_spec,
        out_shape=jax.ShapeDtypeStruct((width, TILE), jnp.float32),
        compiler_params=params(),
        cost_estimate=cost(5),
    )(early_merged)
    residual, five = lax.optimization_barrier((residual, five))
    residual = residual_part(1, [residual])
    summed, residual, *five_x = lax.optimization_barrier((summed, residual, *five_x))
    merged, squares = merge_call([five_x, [early_merged]], 2, distinct=True, merged=1, squared=True)
    total = tensor_sum(squares)
    half_shape = jax.ShapeDtypeStruct((ROWS, WIDE), jnp.float32)
    half_spec = whole(half_shape.shape)
    combined = pl.pallas_call(
        left_kernel,
        grid=(1,),
        in_specs=[whole(merged.shape), pl.BlockSpec((WIDE, TILE), lambda j: (0, 0)), const_spec],
        out_specs=half_spec,
        out_shape=half_shape,
        compiler_params=params(),
        cost_estimate=cost(4),
    )(merged, summed, inverse)
    combined, total = lax.optimization_barrier((combined, total))
    update = pl.pallas_call(
        right_kernel,
        grid=(2,),
        in_specs=[whole(merged.shape), pl.BlockSpec((WIDE, TILE), lambda j: (1, 0)), const_spec, half_spec, whole((8, 128))],
        out_specs=pl.BlockSpec((ROWS, WIDE), lambda j: (0, 1 - j)),
        out_shape=jax.ShapeDtypeStruct((ROWS, width), jnp.float32),
        compiler_params=params(),
        cost_estimate=cost(5),
    )(merged, summed, inverse, combined, total)
    return (update, residual)


def solution(mesh):
    return jax.shard_map(
        shards,
        mesh=mesh,
        in_specs=(P("dp", None, "tensor"), P("dp", None, "tensor"), P("dp", None, "tensor", None)),
        out_specs=(P(None, "tensor"), P("dp", None, "tensor")),
        check_vma=False,
    )
```
